32 devices in a mesh: clip: 4 (over y, core), tm: 2 (over x), height: 4 (over z).
Axes of the slice: x: 2, y: 2, z: 4, core: 2. Of those that a mesh axis runs over, the one named last changes fastest.
Arguments:
- pixels: bfloat16 [16, 3, 4, 4, 384], P('clip', None, 'tm', 'height'), may hold values from -6 to 6
- lengths: int32 [16], replicated, may hold values from 2 to 4, as said below
- route: int32 [16], replicated, may hold values from 0 to 3, as said below
- w_in: bfloat16 [96, 3, 3, 3, 3], replicated, may hold values from -0.625 to 0.625
- b_in: float32 [96], replicated, may hold values from -3 to 3
- gain: float32 [96], replicated, may hold values from 0.1 to 1.9
- w_mid: bfloat16 [96, 96, 3, 3, 3], replicated, may hold values from -0.125 to 0.125
- b_mid: float32 [96], replicated, may hold values from -3 to 3
Outputs:
- features: bfloat16 [16, 96, 4, 4, 384], P('clip', None, 'tm', 'height')
The draws below stay inside these ranges and needn't reach their ends.
Inputs may be any that keep to these rules, and one draw needn't show every extreme that they name: `lengths`: some clip has 4 frames and some clip has 2. `route`: in each aligned block of 4 clips every value 0 to 3 appears exactly once; the lists are chosen from the lengths so that the frame totals of the clip devices are close.
All inputs are finite; a program needn't handle non-finite values.
Results may differ from the reference program's by a relative error of at most 0.009.
Values may be sent and summed in bfloat16 or wider, within the bound.
A program may use at most 64 MiB of HBM per device.

```python
import jax
import jax.numpy as jnp
from jax import lax

CH = 96
C_IN = 3
W_COLS = 384
CLIPS_DEV = 4
CLIPS = 16
FRAMES = 4
ROWS = 4


def clip_plan(key):
    base = jax.random.fold_in(key, 7)
    drawn = jax.random.randint(base, (CLIPS,), 2, FRAMES + 1).astype(jnp.int32)
    drawn = drawn.at[0].set(FRAMES).at[1].set(2)
    blocks = CLIPS // CLIPS_DEV
    grid = drawn.reshape(blocks, CLIPS_DEV)
    within = jnp.arange(CLIPS_DEV, dtype=jnp.int32)[None, :]
    score = grid * CLIPS_DEV + (CLIPS_DEV - 1 - within)
    order = jnp.argsort(-score, axis=1, stable=True).astype(jnp.int32)
    rank = jnp.argsort(order, axis=1, stable=True).astype(jnp.int32)
    block_ids = jnp.arange(blocks, dtype=jnp.int32)[:, None]
    route = (rank + block_ids) % CLIPS_DEV
    return (drawn, route.reshape(CLIPS).astype(jnp.int32))


def draw_lengths(key, part):
    return clip_plan(key)[0]


def draw_route(key, part):
    return clip_plan(key)[1]


def steps_of(own_key, dims, split, least, largest):
    def one(dim, blocks):
        heights = jax.random.uniform(jax.random.fold_in(jax.random.fold_in(own_key, 6), dim), (blocks,), jnp.float32, least / len(split), largest / len(split))
        return jnp.repeat(jnp.exp(heights), dims[dim] // blocks).reshape((-1,) + (1,) * (len(dims) - dim - 1))

    level = one(*split[0])
    for cut in split[1:]:
        level = level * one(*cut)
    return level


def normal_values(stream_key, dims, width, bound, shards=(), kind=jnp.bfloat16):
    entries = width * jax.random.normal(stream_key, dims, jnp.float32)
    if shards:
        entries = entries * steps_of(stream_key, dims, shards, -0.22, 0.18)
    return jnp.clip(entries, -bound, bound).astype(kind)


def setup_inputs(seed: int = 0) -> dict:
    splits = jax.random.split(jax.random.key(seed), 9)
    return {
        "pixels": normal_values(splits[0], (CLIPS, C_IN, FRAMES, ROWS, W_COLS), 1.0, 6.0, ((0, 4), (2, 2), (3, 4))),
        "lengths": draw_lengths(jax.random.fold_in(splits[8], 71), 0),
        "route": draw_route(jax.random.fold_in(splits[8], 71), 0),
        "w_in": normal_values(splits[3], (CH, C_IN, 3, 3, 3), (C_IN * 27) ** -0.5, 0.625),
        "b_in": normal_values(splits[4], (CH,), 0.5, 3.0, (), jnp.float32),
        "gain": jnp.clip(1.0 + 0.18 * jax.random.normal(splits[5], (CH,), jnp.float32), 0.1, 1.9),
        "w_mid": normal_values(splits[6], (CH, CH, 3, 3, 3), (CH * 27) ** -0.5, 0.125),
        "b_mid": normal_values(splits[7], (CH,), 0.5, 3.0, (), jnp.float32),
    }


def causal_conv(clip_data, kernel, bias):
    padded = jnp.pad(clip_data, ((0, 0), (2, 0), (1, 1), (1, 1)))
    result = lax.conv_general_dilated(padded[None], kernel, (1, 1, 1), 'VALID', dimension_numbers=('NCDHW', 'OIDHW', 'NCDHW'), preferred_element_type=jnp.float32)[0]
    return result + bias[:, None, None, None]

def reference(pixels, lengths, route, w_in, b_in, gain, w_mid, b_mid):

    def one_clip(inputs):
        clip_pixels, clip_length = inputs
        stem = causal_conv(clip_pixels, w_in, b_in).astype(jnp.bfloat16)
        stem_wide = stem.astype(jnp.float32)
        scale_inv = lax.rsqrt(lax.optimization_barrier(jnp.mean(stem_wide * stem_wide, axis=0, keepdims=True)) + 1e-06)
        act = jax.nn.silu(stem_wide * scale_inv * gain[:, None, None, None]).astype(jnp.bfloat16)
        block = (causal_conv(act, w_mid, b_mid) + stem_wide).astype(jnp.bfloat16)
        frame_ids = jnp.arange(FRAMES, dtype=jnp.int32)
        keep = (frame_ids < clip_length)[None, :, None, None]
        return jnp.where(keep, block, jnp.zeros_like(block))
    blocks = lax.map(one_clip, (pixels, lengths))
    slots = (route * CLIPS_DEV + jnp.arange(CLIPS, dtype=jnp.int32) // CLIPS_DEV).astype(jnp.int32)
    return jnp.zeros_like(blocks).at[slots].set(blocks)
```

```python
import functools

import jax
import jax.numpy as jnp
from jax import lax
from jax.experimental import pallas as pl
from jax.experimental.pallas import tpu as pltpu
from jax.sharding import PartitionSpec as P

F32, BF16 = jnp.float32, jnp.bfloat16
REACH = (-2, -1, 1, 2)


def gather_kernel(groups, heights, route_ref, pix_ref, out_ref, send, s1, r1, s2, r2):
    clip = lax.axis_index("clip")
    tm = lax.axis_index("tm")
    h = lax.axis_index("height")

    def there(dz):
        return jnp.logical_and(h + dz >= 0, h + dz < heights)

    barrier = pltpu.get_barrier_semaphore()
    for k in range(1, groups):
        pl.semaphore_signal(barrier, inc=1, device_id={"clip": lax.rem(clip + k, groups)})
    pl.semaphore_signal(barrier, inc=1, device_id={"tm": 1 - tm})
    count = groups
    for dz in REACH:
        @pl.when(there(dz))
        def _(dz=dz):
            pl.semaphore_signal(barrier, inc=1, device_id={"height": h + dz})
            pl.semaphore_signal(barrier, inc=1, device_id={"tm": 1 - tm, "height": h + dz})
        count = count + 2 * there(dz).astype(jnp.int32)

    for d in range(groups):
        total = None
        for j in range(groups):
            hit = (route_ref[clip * groups + j] == d).astype(F32)
            term = pix_ref[j].astype(F32) * hit
            total = term if total is None else total + term
        send[d] = total.astype(BF16)
    out_ref[1, 2, clip] = send[clip]
    zero = jnp.zeros(out_ref.shape[2:], BF16)
    for k in range(5):
        lost = jnp.logical_not(there(k - 2))

        @pl.when(jnp.logical_or(lost, tm == 0))
        def _(k=k):
            out_ref[0, k] = zero
        if k != 2:
            @pl.when(lost)
            def _(k=k):
                out_ref[1, k] = zero

    pl.semaphore_wait(barrier, count)
    first = []
    for k in range(1, groups):
        d = lax.rem(clip + k, groups)
        copy = pltpu.make_async_remote_copy(
            send.at[d], out_ref.at[1, 2, clip], s1.at[k], r1.at[k],
            device_id={"clip": d})
        copy.start()
        first.append(copy)
    for k in range(1, groups):
        source = lax.rem(clip + groups - k, groups)
        pltpu.make_async_remote_copy(
            send.at[0], out_ref.at[1, 2, source], s1.at[k], r1.at[k],
            device_id={"clip": source}).wait_recv()

    def out_going(j, dz):
        place = {"height": h + dz} if j == 1 else {"tm": 1 - tm, "height": h + dz}
        return pltpu.make_async_remote_copy(
            out_ref.at[1, 2], out_ref.at[j, 2 - dz], s2.at[j, 2 - dz], r2.at[j, 2 - dz],
            device_id=place)

    def in_coming(j, k):
        return pltpu.make_async_remote_copy(
            out_ref.at[1, 2], out_ref.at[j, k], s2.at[j, k], r2.at[j, k],
            device_id={"tm": 1 - tm})

    hops = [(0, 0)] + [(j, dz) for dz in (1, -1, 2, -2) for j in (0, 1)]
    for j, dz in hops:
        @pl.when(jnp.logical_and(there(dz), jnp.logical_or(j == 1, tm == 0)))
        def _(j=j, dz=dz):
            out_going(j, dz).start()
    for copy in first:
        copy.wait_send()
    for j, dz in hops:
        @pl.when(jnp.logical_and(there(dz), jnp.logical_or(j == 1, tm == 1)))
        def _(j=j, dz=dz):
            in_coming(j, 2 + dz).wait_recv()
    for j, dz in hops:
        @pl.when(jnp.logical_and(there(dz), jnp.logical_or(j == 1, tm == 0)))
        def _(j=j, dz=dz):
            out_going(j, dz).wait_send()


def encode_kernel(groups, heights, lengths_ref, route_ref, pix_ref, w1_ref, par_ref, w2_ref, out_ref, grid, cols, acts, wide):
    ch = par_ref.shape[0]
    width = pix_ref.shape[-1]
    clip = lax.axis_index("clip")
    tm = lax.axis_index("tm")
    h = lax.axis_index("height")
    lane = lax.broadcasted_iota(jnp.int32, (1, width), 1)
    b_in = par_ref[:, 0:1]
    gain = par_ref[:, 1:2]
    b_mid = par_ref[:, 2:3]

    def right(v):
        return jnp.where(lane == 0, 0.0, pltpu.roll(v, 1, 1))

    def left(v):
        return jnp.where(lane == width - 1, 0.0, pltpu.roll(v, width - 1, 1))

    wide[...] = jnp.zeros_like(wide)
    for dt in range(3):
        for dr in range(3):
            for dc in range(3):
                at = (dt * 3 + dr) * 128
                wide[dc * ch:(dc + 1) * ch, at:at + ch] = w2_ref[dt, dr, dc]

    def one(c, carry):
        grid[...] = jnp.zeros_like(grid)
        for j in range(2):
            for k in range(5):
                for f in range(2):
                    grid[2 + 2 * j + f, 3 * k:3 * k + 3, :] = pix_ref[j, k, c, f].astype(F32)
        for p in range(6):
            v = grid[p]
            cols[p * 48:p * 48 + 16, :] = right(v).astype(BF16)
            cols[p * 48 + 16:p * 48 + 32, :] = v.astype(BF16)
            cols[p * 48 + 32:p * 48 + 48, :] = left(v).astype(BF16)
        kept = []
        pad = jnp.zeros((128 - ch, width), BF16)
        for f in range(4):
            s = jnp.dot(w1_ref[...], cols[f * 48:f * 48 + 144, :], preferred_element_type=F32)
            for r in range(3):
                stem = (s[r * ch:(r + 1) * ch] + b_in).astype(BF16).astype(F32)
                scale = lax.rsqrt(jnp.mean(stem * stem, axis=0, keepdims=True) + 1e-6)
                v = 0.5 * (stem * scale * gain)
                act = v + v * jnp.tanh(v)
                live = jnp.logical_and(h - 1 + r >= 0, h - 1 + r < heights)
                if f < 2:
                    live = jnp.logical_and(live, tm > 0)
                at = (f * 3 + r) * 128
                acts[at:at + ch, :] = jnp.where(live, act, 0.0).astype(BF16)
                acts[at + ch:at + 128, :] = pad
                if f >= 2 and r == 1:
                    kept.append(stem)
        length = 0
        for j in range(groups):
            q = c * groups + j
            length = length + jnp.where(route_ref[q] == clip, lengths_ref[q], 0)
        for t in range(2):
            y = jnp.dot(wide[...], acts[t * 384:t * 384 + 1152, :], preferred_element_type=F32)
            o = y[ch:2 * ch] + right(y[:ch]) + left(y[2 * ch:]) + b_mid + kept[t]
            out_ref[c, t] = jnp.where(tm * 2 + t < length, o, 0.0).astype(BF16)
        return carry

    lax.fori_loop(0, groups, one, 0)


def local(groups, heights, pixels, lengths, route, w_in, b_in, gain, w_mid, b_mid):
    clips, colours, frames, _, width = pixels.shape
    ch = w_in.shape[0]
    vmem = pl.BlockSpec(memory_space=pltpu.VMEM)
    smem = pl.BlockSpec(memory_space=pltpu.SMEM)
    pix = jnp.transpose(pixels[:, :, :, 0, :], (0, 2, 1, 3))
    around = pl.pallas_call(
        functools.partial(gather_kernel, groups, heights),
        out_shape=jax.ShapeDtypeStruct((2, 5, clips, frames, colours, width), BF16),
        in_specs=[smem, vmem],
        out_specs=vmem,
        scratch_shapes=[
            pltpu.VMEM((groups, frames, colours, width), BF16),
            pltpu.SemaphoreType.DMA((groups,)),
            pltpu.SemaphoreType.DMA((groups,)),
            pltpu.SemaphoreType.DMA((2, 5)),
            pltpu.SemaphoreType.DMA((2, 5)),
        ],
        compiler_params=pltpu.CompilerParams(collective_id=0, has_side_effects=True),
    )(route, pix)
    taps = jnp.transpose(w_in, (0, 2, 4, 3, 1)).reshape(ch, 3, 3, 9)
    w1 = jnp.concatenate(
        [jnp.pad(taps, ((0, 0), (0, 0), (0, 0), (3 * r, 7 - 3 * r))).reshape(ch, 144) for r in range(3)], axis=0)
    par = jnp.stack([b_in, gain, b_mid], axis=1)
    w2 = jnp.transpose(w_mid, (2, 3, 4, 0, 1))
    out = pl.pallas_call(
        functools.partial(encode_kernel, groups, heights),
        out_shape=jax.ShapeDtypeStruct((clips, frames, ch, width), BF16),
        in_specs=[smem, smem, vmem, vmem, vmem, vmem],
        out_specs=vmem,
        scratch_shapes=[
            pltpu.VMEM((6, 16, width), F32),
            pltpu.VMEM((288, width), BF16),
            pltpu.VMEM((12 * 128, width), BF16),
            pltpu.VMEM((3 * ch, 9 * 128), BF16),
        ],
        compiler_params=pltpu.CompilerParams(vmem_limit_bytes=32 * 1024 * 1024),
    )(lengths, route, around, w1, par, w2)
    return jnp.transpose(out, (0, 2, 1, 3))[:, :, :, None, :]


def solution(mesh):
    placed = (P("clip", None, "tm", "height", None), P(), P(), P(), P(), P(), P(), P())
    return jax.shard_map(
        functools.partial(local, mesh.shape["clip"], mesh.shape["height"]),
        mesh=mesh,
        in_specs=placed,
        out_specs=P("clip", None, "tm", "height", None),
        check_vma=False,
    )
```

```python
import functools

import jax
import jax.numpy as jnp
from jax import lax
from jax.experimental import pallas as pl
from jax.experimental.pallas import tpu as pltpu
from jax.sharding import PartitionSpec as P

F32, BF16 = jnp.float32, jnp.bfloat16
REACH = (-2, -1, 1, 2)


def gather_kernel(groups, heights, route_ref, pix_ref, out_ref, send, s1, r1, s2, r2):
    clip = lax.axis_index("clip")
    tm = lax.axis_index("tm")
    h = lax.axis_index("height")

    def there(dz):
        return jnp.logical_and(h + dz >= 0, h + dz < heights)

    barrier = pltpu.get_barrier_semaphore()
    for k in range(1, groups):
        pl.semaphore_signal(barrier, inc=1, device_id={"clip": lax.rem(clip + k, groups)})
    pl.semaphore_signal(barrier, inc=1, device_id={"tm": 1 - tm})
    count = groups
    for dz in REACH:
        @pl.when(there(dz))
        def _(dz=dz):
            pl.semaphore_signal(barrier, inc=1, device_id={"height": h + dz})
            pl.semaphore_signal(barrier, inc=1, device_id={"tm": 1 - tm, "height": h + dz})
        count = count + 2 * there(dz).astype(jnp.int32)

    for d in range(groups):
        total = None
        for j in range(groups):
            hit = (route_ref[clip * groups + j] == d).astype(F32)
            term = pix_ref[j].astype(F32) * hit
            total = term if total is None else total + term
        for f in range(total.shape[1]):
            send[d, f] = total[:, f, :].astype(BF16)
    out_ref[1, 2, clip] = send[clip]
    zero = jnp.zeros(out_ref.shape[2:], BF16)
    for k in range(5):
        lost = jnp.logical_not(there(k - 2))

        @pl.when(jnp.logical_or(lost, tm == 0))
        def _(k=k):
            out_ref[0, k] = zero
        if k != 2:
            @pl.when(lost)
            def _(k=k):
                out_ref[1, k] = zero

    pl.semaphore_wait(barrier, count)
    first = []
    for k in range(1, groups):
        d = lax.rem(clip + k, groups)
        copy = pltpu.make_async_remote_copy(
            send.at[d], out_ref.at[1, 2, clip], s1.at[k], r1.at[k],
            device_id={"clip": d})
        copy.start()
        first.append(copy)
    for k in range(1, groups):
        source = lax.rem(clip + groups - k, groups)
        pltpu.make_async_remote_copy(
            send.at[0], out_ref.at[1, 2, source], s1.at[k], r1.at[k],
            device_id={"clip": source}).wait_recv()

    def out_going(j, dz):
        place = {"height": h + dz} if j == 1 else {"tm": 1 - tm, "height": h + dz}
        return pltpu.make_async_remote_copy(
            out_ref.at[1, 2], out_ref.at[j, 2 - dz], s2.at[j, 2 - dz], r2.at[j, 2 - dz],
            device_id=place)

    def in_coming(j, k):
        return pltpu.make_async_remote_copy(
            out_ref.at[1, 2], out_ref.at[j, k], s2.at[j, k], r2.at[j, k],
            device_id={"tm": 1 - tm})

    hops = [(0, 0)] + [(j, dz) for dz in (1, -1, 2, -2) for j in (0, 1)]
    for j, dz in hops:
        @pl.when(jnp.logical_and(there(dz), jnp.logical_or(j == 1, tm == 0)))
        def _(j=j, dz=dz):
            out_going(j, dz).start()
    for copy in first:
        copy.wait_send()
    for j, dz in hops:
        @pl.when(jnp.logical_and(there(dz), jnp.logical_or(j == 1, tm == 1)))
        def _(j=j, dz=dz):
            in_coming(j, 2 + dz).wait_recv()
    for j, dz in hops:
        @pl.when(jnp.logical_and(there(dz), jnp.logical_or(j == 1, tm == 0)))
        def _(j=j, dz=dz):
            out_going(j, dz).wait_send()


def encode_kernel(groups, heights, lengths_ref, route_ref, pix_ref, taps_ref, b_in_ref, gain_ref, b_mid_ref, w2_ref, out_ref,
                  grid, cols, acts, wide, tall, w1_ref, rows):
    ch = b_in_ref.shape[1]
    width = pix_ref.shape[-1]
    clip = lax.axis_index("clip")
    tm = lax.axis_index("tm")
    h = lax.axis_index("height")
    lane = lax.broadcasted_iota(jnp.int32, (1, width), 1)
    rows[...] = jnp.zeros_like(rows)
    for n, row in enumerate((b_in_ref, gain_ref, b_mid_ref)):
        rows[n:n + 1, :ch] = row[...]
    par = rows[...].T[:ch]
    b_in, gain, b_mid = par[:, 0:1], par[:, 1:2], par[:, 2:3]

    def right(v):
        return jnp.where(lane == 0, 0.0, pltpu.roll(v, 1, 1))

    def left(v):
        return jnp.where(lane == width - 1, 0.0, pltpu.roll(v, width - 1, 1))

    tall[...] = jnp.zeros_like(tall)
    for i in range(3):
        for dt in range(3):
            for dr in range(3):
                piece = taps_ref[i, dt, dr].astype(F32)
                for r in range(3):
                    for dc in range(3):
                        at = dt * 48 + dc * 16 + (r + dr) * 3 + i
                        tall[at:at + 1, r * 128:r * 128 + ch] = piece[dc:dc + 1]
    for r in range(3):
        w1_ref[r * ch:(r + 1) * ch, :] = tall[:, r * 128:(r + 1) * 128].T[:ch].astype(BF16)
    wide[...] = jnp.zeros_like(wide)
    for dt in range(3):
        for dr in range(3):
            for dc in range(3):
                at = (dt * 3 + dr) * 128
                wide[dc * ch:(dc + 1) * ch, at:at + ch] = w2_ref[dt, dr, dc]

    def one(c, carry):
        grid[...] = jnp.zeros_like(grid)
        for j in range(2):
            for k in range(5):
                for f in range(2):
                    grid[2 + 2 * j + f, 3 * k:3 * k + 3, :] = pix_ref[j, k, c, f].astype(F32)
        for p in range(6):
            v = grid[p]
            cols[p * 48:p * 48 + 16, :] = right(v).astype(BF16)
            cols[p * 48 + 16:p * 48 + 32, :] = v.astype(BF16)
            cols[p * 48 + 32:p * 48 + 48, :] = left(v).astype(BF16)
        kept = []
        pad = jnp.zeros((128 - ch, width), BF16)
        for f in range(4):
            s = jnp.dot(w1_ref[...], cols[f * 48:f * 48 + 144, :], preferred_element_type=F32)
            for r in range(3):
                stem = (s[r * ch:(r + 1) * ch] + b_in).astype(BF16).astype(F32)
                scale = lax.rsqrt(jnp.mean(stem * stem, axis=0, keepdims=True) + 1e-6)
                v = 0.5 * (stem * scale * gain)
                act = v + v * jnp.tanh(v)
                live = jnp.logical_and(h - 1 + r >= 0, h - 1 + r < heights)
                if f < 2:
                    live = jnp.logical_and(live, tm > 0)
                at = (f * 3 + r) * 128
                acts[at:at + ch, :] = jnp.where(live, act, 0.0).astype(BF16)
                acts[at + ch:at + 128, :] = pad
                if f >= 2 and r == 1:
                    kept.append(stem)
        length = 0
        for j in range(groups):
            q = c * groups + j
            length = length + jnp.where(route_ref[q] == clip, lengths_ref[q], 0)
        for t in range(2):
            y = jnp.dot(wide[...], acts[t * 384:t * 384 + 1152, :], preferred_element_type=F32)
            o = y[ch:2 * ch] + right(y[:ch]) + left(y[2 * ch:]) + b_mid + kept[t]
            out_ref[c, t] = jnp.where(tm * 2 + t < length, o, 0.0).astype(BF16)
        return carry

    lax.fori_loop(0, groups, one, 0)


def local(groups, heights, pixels, lengths, route, w_in, b_in, gain, w_mid, b_mid):
    clips, colours, frames, _, width = pixels.shape
    ch = w_in.shape[0]
    vmem = pl.BlockSpec(memory_space=pltpu.VMEM)
    smem = pl.BlockSpec(memory_space=pltpu.SMEM)
    pix = pixels.reshape(clips, colours, frames, width)
    around = pl.pallas_call(
        functools.partial(gather_kernel, groups, heights),
        out_shape=jax.ShapeDtypeStruct((2, 5, clips, frames, colours, width), BF16),
        in_specs=[smem, vmem],
        out_specs=vmem,
        scratch_shapes=[
            pltpu.VMEM((groups, frames, colours, width), BF16),
            pltpu.SemaphoreType.DMA((groups,)),
            pltpu.SemaphoreType.DMA((groups,)),
            pltpu.SemaphoreType.DMA((2, 5)),
            pltpu.SemaphoreType.DMA((2, 5)),
        ],
        compiler_params=pltpu.CompilerParams(collective_id=0, has_side_effects=True),
    )(route, pix)
    w1 = jnp.transpose(w_in, (1, 2, 3, 4, 0))
    rows = [v.reshape(1, ch) for v in (b_in, gain, b_mid)]
    w2 = jnp.transpose(w_mid, (2, 3, 4, 0, 1))
    out = pl.pallas_call(
        functools.partial(encode_kernel, groups, heights),
        out_shape=jax.ShapeDtypeStruct((clips, frames, ch, width), BF16),
        in_specs=[smem, smem] + [vmem] * 6,
        out_specs=vmem,
        scratch_shapes=[
            pltpu.VMEM((6, 16, width), F32),
            pltpu.VMEM((288, width), BF16),
            pltpu.VMEM((12 * 128, width), BF16),
            pltpu.VMEM((3 * ch, 9 * 128), BF16),
            pltpu.VMEM((144, 3 * 128), F32),
            pltpu.VMEM((3 * ch, 144), BF16),
            pltpu.VMEM((8, 128), F32),
        ],
        compiler_params=pltpu.CompilerParams(vmem_limit_bytes=32 * 1024 * 1024),
    )(lengths, route, around, w1, *rows, w2)
    return jnp.transpose(out, (0, 2, 1, 3))[:, :, :, None, :]


def solution(mesh):
    placed = (P("clip", None, "tm", "height", None), P(), P(), P(), P(), P(), P(), P())
    return jax.shard_map(
        functools.partial(local, mesh.shape["clip"], mesh.shape["height"]),
        mesh=mesh,
        in_specs=placed,
        out_specs=P("clip", None, "tm", "height", None),
        check_vma=False,
    )
```

```python
import functools

import jax
import jax.numpy as jnp
from jax import lax
from jax.experimental import pallas as pl
from jax.experimental.pallas import tpu as pltpu
from jax.sharding import PartitionSpec as P

F32, BF16 = jnp.float32, jnp.bfloat16
REACH = (-2, -1, 1, 2)


def gather(groups, heights, prepare, route_ref, pix_ref, out_ref, send, s1, r1, s2, r2):
    clip = lax.axis_index("clip")
    tm = lax.axis_index("tm")
    h = lax.axis_index("height")

    def there(dz):
        return jnp.logical_and(h + dz >= 0, h + dz < heights)

    barrier = pltpu.get_barrier_semaphore()
    for k in range(1, groups):
        pl.semaphore_signal(barrier, inc=1, device_id={"clip": lax.rem(clip + k, groups)})
    pl.semaphore_signal(barrier, inc=1, device_id={"tm": 1 - tm})
    count = groups
    for dz in REACH:
        @pl.when(there(dz))
        def _(dz=dz):
            pl.semaphore_signal(barrier, inc=1, device_id={"height": h + dz})
            pl.semaphore_signal(barrier, inc=1, device_id={"tm": 1 - tm, "height": h + dz})
        count = count + 2 * there(dz).astype(jnp.int32)

    for d in range(groups):
        total = None
        for j in range(groups):
            hit = (route_ref[clip * groups + j] == d).astype(F32)
            term = pix_ref[j].astype(F32) * hit
            total = term if total is None else total + term
        for f in range(total.shape[1]):
            send[d, f] = total[:, f, :].astype(BF16)
    out_ref[1, 2, clip] = send[clip]
    zero = jnp.zeros(out_ref.shape[2:], BF16)
    for k in range(5):
        lost = jnp.logical_not(there(k - 2))

        @pl.when(jnp.logical_or(lost, tm == 0))
        def _(k=k):
            out_ref[0, k] = zero
        if k != 2:
            @pl.when(lost)
            def _(k=k):
                out_ref[1, k] = zero

    pl.semaphore_wait(barrier, count)
    first = []
    for k in range(1, groups):
        d = lax.rem(clip + k, groups)
        copy = pltpu.make_async_remote_copy(
            send.at[d], out_ref.at[1, 2, clip], s1.at[k], r1.at[k],
            device_id={"clip": d})
        copy.start()
        first.append(copy)
    for k in range(1, groups):
        source = lax.rem(clip + groups - k, groups)
        pltpu.make_async_remote_copy(
            send.at[0], out_ref.at[1, 2, source], s1.at[k], r1.at[k],
            device_id={"clip": source}).wait_recv()

    def out_going(j, dz):
        place = {"height": h + dz} if j == 1 else {"tm": 1 - tm, "height": h + dz}
        return pltpu.make_async_remote_copy(
            out_ref.at[1, 2], out_ref.at[j, 2 - dz], s2.at[j, 2 - dz], r2.at[j, 2 - dz],
            device_id=place)

    def in_coming(j, k):
        return pltpu.make_async_remote_copy(
            out_ref.at[1, 2], out_ref.at[j, k], s2.at[j, k], r2.at[j, k],
            device_id={"tm": 1 - tm})

    hops = [(0, 0)] + [(j, dz) for dz in (1, -1, 2, -2) for j in (0, 1)]
    for j, dz in hops:
        @pl.when(jnp.logical_and(there(dz), jnp.logical_or(j == 1, tm == 0)))
        def _(j=j, dz=dz):
            out_going(j, dz).start()
    prepare()
    for copy in first:
        copy.wait_send()
    for j, dz in hops:
        @pl.when(jnp.logical_and(there(dz), jnp.logical_or(j == 1, tm == 1)))
        def _(j=j, dz=dz):
            in_coming(j, 2 + dz).wait_recv()
    for j, dz in hops:
        @pl.when(jnp.logical_and(there(dz), jnp.logical_or(j == 1, tm == 0)))
        def _(j=j, dz=dz):
            out_going(j, dz).wait_send()


def kernel(groups, heights, lengths_ref, route_ref, own_ref, taps_hbm, b_in_ref, gain_ref, b_mid_ref, w2_hbm, out_ref,
           pix_ref, taps_ref, w2_ref, grid, cols, acts, wide, tall, w1_ref, rows, loaded, *sent):
    load_taps = pltpu.make_async_copy(taps_hbm, taps_ref, loaded.at[0])
    load_w2 = pltpu.make_async_copy(w2_hbm, w2_ref, loaded.at[1])
    load_taps.start()
    load_w2.start()
    ch = b_in_ref.shape[1]
    width = pix_ref.shape[-1]
    clip = lax.axis_index("clip")
    tm = lax.axis_index("tm")
    h = lax.axis_index("height")
    lane = lax.broadcasted_iota(jnp.int32, (1, width), 1)
    rows[...] = jnp.zeros_like(rows)
    for n, row in enumerate((b_in_ref, gain_ref, b_mid_ref)):
        rows[n:n + 1, :ch] = row[...]
    par = rows[...].T[:ch]
    b_in, gain, b_mid = par[:, 0:1], par[:, 1:2], par[:, 2:3]

    def right(v):
        return jnp.where(lane == 0, 0.0, pltpu.roll(v, 1, 1))

    def left(v):
        return jnp.where(lane == width - 1, 0.0, pltpu.roll(v, width - 1, 1))

    def prepare():
        load_taps.wait()
        tall[...] = jnp.zeros_like(tall)
        for i in range(3):
            for dt in range(3):
                for dr in range(3):
                    piece = taps_ref[i, dt, dr].astype(F32)
                    for r in range(3):
                        for dc in range(3):
                            at = dt * 48 + dc * 16 + (r + dr) * 3 + i
                            tall[at:at + 1, r * 128:r * 128 + ch] = piece[dc:dc + 1]
        for r in range(3):
            w1_ref[r * ch:(r + 1) * ch, :] = tall[:, r * 128:(r + 1) * 128].T[:ch].astype(BF16)
        load_w2.wait()
        wide[...] = jnp.zeros_like(wide)
        for dt in range(3):
            for dr in range(3):
                for dc in range(3):
                    at = (dt * 3 + dr) * 128
                    wide[dc * ch:(dc + 1) * ch, at:at + ch] = w2_ref[dt, dr, dc]

    gather(groups, heights, prepare, route_ref, own_ref, pix_ref, *sent)

    def one(c, carry):
        grid[...] = jnp.zeros_like(grid)
        for j in range(2):
            for k in range(5):
                for f in range(2):
                    grid[2 + 2 * j + f, 3 * k:3 * k + 3, :] = pix_ref[j, k, c, f].astype(F32)
        for p in range(6):
            v = grid[p]
            cols[p * 48:p * 48 + 16, :] = right(v).astype(BF16)
            cols[p * 48 + 16:p * 48 + 32, :] = v.astype(BF16)
            cols[p * 48 + 32:p * 48 + 48, :] = left(v).astype(BF16)
        kept = []
        pad = jnp.zeros((128 - ch, width), BF16)
        for f in range(4):
            s = jnp.dot(w1_ref[...], cols[f * 48:f * 48 + 144, :], preferred_element_type=F32)
            for r in range(3):
                stem = (s[r * ch:(r + 1) * ch] + b_in).astype(BF16).astype(F32)
                scale = lax.rsqrt(jnp.mean(stem * stem, axis=0, keepdims=True) + 1e-6)
                v = 0.5 * (stem * scale * gain)
                act = v + v * jnp.tanh(v)
                live = jnp.logical_and(h - 1 + r >= 0, h - 1 + r < heights)
                if f < 2:
                    live = jnp.logical_and(live, tm > 0)
                at = (f * 3 + r) * 128
                acts[at:at + ch, :] = jnp.where(live, act, 0.0).astype(BF16)
                acts[at + ch:at + 128, :] = pad
                if f >= 2 and r == 1:
                    kept.append(stem)
        length = 0
        for j in range(groups):
            q = c * groups + j
            length = length + jnp.where(route_ref[q] == clip, lengths_ref[q], 0)
        for t in range(2):
            y = jnp.dot(wide[...], acts[t * 384:t * 384 + 1152, :], preferred_element_type=F32)
            o = y[ch:2 * ch] + right(y[:ch]) + left(y[2 * ch:]) + b_mid + kept[t]
            out_ref[c, t] = jnp.where(tm * 2 + t < length, o, 0.0).astype(BF16)
        return carry

    lax.fori_loop(0, groups, one, 0)


def local(groups, heights, pixels, lengths, route, w_in, b_in, gain, w_mid, b_mid):
    clips, colours, frames, _, width = pixels.shape
    ch = w_in.shape[0]
    vmem = pl.BlockSpec(memory_space=pltpu.VMEM)
    hbm = pl.BlockSpec(memory_space=pltpu.HBM)
    smem = pl.BlockSpec(memory_space=pltpu.SMEM)
    pix = pixels.reshape(clips, colours, frames, width)
    w1 = jnp.transpose(w_in, (1, 2, 3, 4, 0))
    rows = [v.reshape(1, ch) for v in (b_in, gain, b_mid)]
    w2 = jnp.transpose(w_mid, (2, 3, 4, 0, 1))
    out = pl.pallas_call(
        functools.partial(kernel, groups, heights),
        out_shape=jax.ShapeDtypeStruct((clips, frames, ch, width), BF16),
        in_specs=[smem, smem, vmem, hbm, vmem, vmem, vmem, hbm],
        out_specs=vmem,
        scratch_shapes=[
            pltpu.VMEM((2, 5, clips, frames, colours, width), BF16),
            pltpu.VMEM(w1.shape, BF16),
            pltpu.VMEM(w2.shape, BF16),
            pltpu.VMEM((6, 16, width), F32),
            pltpu.VMEM((288, width), BF16),
            pltpu.VMEM((12 * 128, width), BF16),
            pltpu.VMEM((3 * ch, 9 * 128), BF16),
            pltpu.VMEM((144, 3 * 128), F32),
            pltpu.VMEM((3 * ch, 144), BF16),
            pltpu.VMEM((8, 128), F32),
            pltpu.SemaphoreType.DMA((2,)),
            pltpu.VMEM((groups, frames, colours, width), BF16),
            pltpu.SemaphoreType.DMA((groups,)),
            pltpu.SemaphoreType.DMA((groups,)),
            pltpu.SemaphoreType.DMA((2, 5)),
            pltpu.SemaphoreType.DMA((2, 5)),
        ],
        compiler_params=pltpu.CompilerParams(collective_id=0, has_side_effects=True, vmem_limit_bytes=60 * 1024 * 1024),
    )(lengths, route, pix, w1, *rows, w2)
    return jnp.transpose(out, (0, 2, 1, 3))[:, :, :, None, :]


def solution(mesh):
    placed = (P("clip", None, "tm", "height", None), P(), P(), P(), P(), P(), P(), P())
    return jax.shard_map(
        functools.partial(local, mesh.shape["clip"], mesh.shape["height"]),
        mesh=mesh,
        in_specs=placed,
        out_specs=P("clip", None, "tm", "height", None),
        check_vma=False,
    )
```

```python
import functools

import jax
import jax.numpy as jnp
from jax import lax
from jax.experimental import pallas as pl
from jax.experimental.pallas import tpu as pltpu
from jax.sharding import PartitionSpec as P

F32, BF16 = jnp.float32, jnp.bfloat16
REACH = (-2, -1, 1, 2)


def gather(groups, heights, prepare, route_ref, pix_ref, out_ref, send, s1, r1, s2, r2):
    clip = lax.axis_index("clip")
    tm = lax.axis_index("tm")
    h = lax.axis_index("height")

    def there(dz):
        return jnp.logical_and(h + dz >= 0, h + dz < heights)

    barrier = pltpu.get_barrier_semaphore()
    for k in range(1, groups):
        pl.semaphore_signal(barrier, inc=1, device_id={"clip": lax.rem(clip + k, groups)})
    pl.semaphore_signal(barrier, inc=1, device_id={"tm": 1 - tm})
    count = groups
    for dz in REACH:
        @pl.when(there(dz))
        def _(dz=dz):
            pl.semaphore_signal(barrier, inc=1, device_id={"height": h + dz})
            pl.semaphore_signal(barrier, inc=1, device_id={"tm": 1 - tm, "height": h + dz})
        count = count + 2 * there(dz).astype(jnp.int32)

    for d in range(groups):
        total = None
        for j in range(groups):
            hit = (route_ref[clip * groups + j] == d).astype(F32)
            term = pix_ref[j].astype(F32) * hit
            total = term if total is None else total + term
        for f in range(total.shape[1]):
            send[d, f] = total[:, f, :].astype(BF16)
    out_ref[1, 2, clip] = send[clip]
    zero = jnp.zeros(out_ref.shape[2:], BF16)
    for k in range(5):
        lost = jnp.logical_not(there(k - 2))

        @pl.when(jnp.logical_or(lost, tm == 0))
        def _(k=k):
            out_ref[0, k] = zero
        if k != 2:
            @pl.when(lost)
            def _(k=k):
                out_ref[1, k] = zero

    pl.semaphore_wait(barrier, count)
    first = []
    for k in range(1, groups):
        d = lax.rem(clip + k, groups)
        copy = pltpu.make_async_remote_copy(
            send.at[d], out_ref.at[1, 2, clip], s1.at[k], r1.at[k],
            device_id={"clip": d})
        copy.start()
        first.append(copy)
    for k in range(1, groups):
        source = lax.rem(clip + groups - k, groups)
        pltpu.make_async_remote_copy(
            send.at[0], out_ref.at[1, 2, source], s1.at[k], r1.at[k],
            device_id={"clip": source}).wait_recv()

    def out_going(j, dz):
        place = {"height": h + dz} if j == 1 else {"tm": 1 - tm, "height": h + dz}
        return pltpu.make_async_remote_copy(
            out_ref.at[1, 2], out_ref.at[j, 2 - dz], s2.at[j, 2 - dz], r2.at[j, 2 - dz],
            device_id=place)

    def in_coming(j, k):
        return pltpu.make_async_remote_copy(
            out_ref.at[1, 2], out_ref.at[j, k], s2.at[j, k], r2.at[j, k],
            device_id={"tm": 1 - tm})

    hops = [(0, 0)] + [(j, dz) for dz in (1, -1, 2, -2) for j in (0, 1)]
    for j, dz in hops:
        @pl.when(jnp.logical_and(there(dz), jnp.logical_or(j == 1, tm == 0)))
        def _(j=j, dz=dz):
            out_going(j, dz).start()
    prepare()
    for copy in first:
        copy.wait_send()
    for j, dz in hops:
        @pl.when(jnp.logical_and(there(dz), jnp.logical_or(j == 1, tm == 1)))
        def _(j=j, dz=dz):
            in_coming(j, 2 + dz).wait_recv()
    for j, dz in hops:
        @pl.when(jnp.logical_and(there(dz), jnp.logical_or(j == 1, tm == 0)))
        def _(j=j, dz=dz):
            out_going(j, dz).wait_send()


def kernel(groups, heights, lengths_ref, route_ref, own_ref, taps_hbm, b_in_ref, gain_ref, b_mid_ref, w2_hbm, out_ref,
           pix_ref, taps_ref, w2_ref, grid, cols, acts, wide, tall, w1_ref, rows, loaded, *sent):
    load_taps = pltpu.make_async_copy(taps_hbm, taps_ref, loaded.at[0])
    load_w2 = pltpu.make_async_copy(w2_hbm, w2_ref, loaded.at[1])
    load_taps.start()
    load_w2.start()
    ch = b_in_ref.shape[1]
    width = pix_ref.shape[-1]
    clip = lax.axis_index("clip")
    tm = lax.axis_index("tm")
    h = lax.axis_index("height")
    lane = lax.broadcasted_iota(jnp.int32, (1, width), 1)
    rows[...] = jnp.zeros_like(rows)
    for n, row in enumerate((b_in_ref, gain_ref, b_mid_ref)):
        rows[n:n + 1, :ch] = row[...]
    par = rows[...].T[:ch]
    b_in, gain, b_mid = par[:, 0:1], par[:, 1:2], par[:, 2:3]

    def right(v):
        return jnp.where(lane == 0, 0.0, pltpu.roll(v, 1, 1))

    def left(v):
        return jnp.where(lane == width - 1, 0.0, pltpu.roll(v, width - 1, 1))

    def prepare():
        load_taps.wait()
        tall[...] = jnp.zeros_like(tall)
        for i in range(3):
            for dt in range(3):
                for dr in range(3):
                    piece = taps_ref[i, dt, dr].astype(F32)
                    for r in range(3):
                        for dc in range(3):
                            at = dt * 48 + dc * 16 + (r + dr) * 3 + i
                            tall[at:at + 1, r * 128:r * 128 + ch] = piece[dc:dc + 1]
        for r in range(3):
            w1_ref[r * ch:(r + 1) * ch, :] = tall[:, r * 128:(r + 1) * 128].T[:ch].astype(BF16)
        load_w2.wait()
        wide[...] = jnp.zeros_like(wide)
        for dt in range(3):
            for dr in range(3):
                for dc in range(3):
                    at = (dt * 3 + dr) * 128
                    wide[dc * ch:(dc + 1) * ch, at:at + ch] = w2_ref[dt, dr, dc]

    gather(groups, heights, prepare, route_ref, own_ref, pix_ref, *sent)

    def one(c, carry):
        grid[...] = jnp.zeros_like(grid)
        for j in range(2):
            for k in range(5):
                for f in range(2):
                    grid[2 + 2 * j + f, 3 * k:3 * k + 3, :] = pix_ref[j, k, c, f].astype(F32)
        for p in range(6):
            v = grid[p]
            cols[p * 48:p * 48 + 16, :] = right(v).astype(BF16)
            cols[p * 48 + 16:p * 48 + 32, :] = v.astype(BF16)
            cols[p * 48 + 32:p * 48 + 48, :] = left(v).astype(BF16)
        kept = []
        pad = jnp.zeros((128 - ch, width), BF16)
        for f in range(4):
            s = jnp.dot(w1_ref[...], cols[f * 48:f * 48 + 144, :], preferred_element_type=F32)
            for r in range(3):
                stem = (s[r * ch:(r + 1) * ch] + b_in).astype(BF16).astype(F32)
                scale = lax.rsqrt(jnp.mean(stem * stem, axis=0, keepdims=True) + 1e-6)
                v = 0.5 * (stem * scale * gain)
                act = v + v * jnp.tanh(v)
                live = jnp.logical_and(h - 1 + r >= 0, h - 1 + r < heights)
                if f < 2:
                    live = jnp.logical_and(live, tm > 0)
                at = (f * 3 + r) * 128
                acts[at:at + ch, :] = jnp.where(live, act, 0.0).astype(BF16)
                acts[at + ch:at + 128, :] = pad
                if f >= 2 and r == 1:
                    kept.append(stem)
        length = 0
        for j in range(groups):
            q = c * groups + j
            length = length + jnp.where(route_ref[q] == clip, lengths_ref[q], 0)
        for t in range(2):
            y = jnp.dot(wide[...], acts[t * 384:t * 384 + 1152, :], preferred_element_type=F32)
            o = y[ch:2 * ch] + right(y[:ch]) + left(y[2 * ch:]) + b_mid + kept[t]
            out_ref[c, t] = jnp.where(tm * 2 + t < length, o, 0.0).astype(BF16)
        return carry

    lax.fori_loop(0, groups, one, 0)


def local(groups, heights, pixels, lengths, route, w_in, b_in, gain, w_mid, b_mid):
    clips, colours, frames, _, width = pixels.shape
    ch = w_in.shape[0]
    vmem = pl.BlockSpec(memory_space=pltpu.VMEM)
    hbm = pl.BlockSpec(memory_space=pltpu.HBM)
    smem = pl.BlockSpec(memory_space=pltpu.SMEM)
    pix = pixels.reshape(clips, colours, frames, width)
    w1 = jnp.transpose(w_in, (1, 2, 3, 4, 0))
    rows = [v.reshape(1, ch) for v in (b_in, gain, b_mid)]
    w2 = jnp.transpose(w_mid, (2, 3, 4, 0, 1))
    out = pl.pallas_call(
        functools.partial(kernel, groups, heights),
        out_shape=jax.ShapeDtypeStruct((clips, frames, ch, width), BF16),
        in_specs=[smem, smem, vmem, hbm, vmem, vmem, vmem, hbm],
        out_specs=vmem,
        scratch_shapes=[
            pltpu.VMEM((2, 5, clips, frames, colours, width), BF16),
            pltpu.VMEM(w1.shape, BF16),
            pltpu.VMEM(w2.shape, BF16),
            pltpu.VMEM((6, 16, width), F32),
            pltpu.VMEM((288, width), BF16),
            pltpu.VMEM((12 * 128, width), BF16),
            pltpu.VMEM((3 * ch, 9 * 128), BF16),
            pltpu.VMEM((144, 3 * 128), F32),
            pltpu.VMEM((3 * ch, 144), BF16),
            pltpu.VMEM((8, 128), F32),
            pltpu.SemaphoreType.DMA((2,)),
            pltpu.VMEM((groups, frames, colours, width), BF16),
            pltpu.SemaphoreType.DMA((groups,)),
            pltpu.SemaphoreType.DMA((groups,)),
            pltpu.SemaphoreType.DMA((2, 5)),
            pltpu.SemaphoreType.DMA((2, 5)),
        ],
        compiler_params=pltpu.CompilerParams(collective_id=0, has_side_effects=True, vmem_limit_bytes=54208 * 1024),
    )(lengths, route, pix, w1, *rows, w2)
    return jnp.transpose(out, (0, 2, 1, 3))[:, :, :, None, :]


def solution(mesh):
    placed = (P("clip", None, "tm", "height", None), P(), P(), P(), P(), P(), P(), P())
    return jax.shard_map(
        functools.partial(local, mesh.shape["clip"], mesh.shape["height"]),
        mesh=mesh,
        in_specs=placed,
        out_specs=P("clip", None, "tm", "height", None),
        check_vma=False,
    )
```

```python
import functools

import jax
import jax.numpy as jnp
from jax import lax
from jax.experimental import pallas as pl
from jax.experimental.pallas import tpu as pltpu
from jax.sharding import PartitionSpec as P

F32, BF16 = jnp.float32, jnp.bfloat16
REACH = (-2, -1, 1, 2)


def gather(groups, heights, prepare, route_ref, pix_ref, out_ref, send, s1, r1, s2, r2):
    clip = lax.axis_index("clip")
    tm = lax.axis_index("tm")
    h = lax.axis_index("height")

    def there(dz):
        return jnp.logical_and(h + dz >= 0, h + dz < heights)

    barrier = pltpu.get_barrier_semaphore()
    for k in range(1, groups):
        pl.semaphore_signal(barrier, inc=1, device_id={"clip": lax.rem(clip + k, groups)})
    pl.semaphore_signal(barrier, inc=1, device_id={"tm": 1 - tm})
    count = groups
    for dz in REACH:
        @pl.when(there(dz))
        def _(dz=dz):
            pl.semaphore_signal(barrier, inc=1, device_id={"height": h + dz})
            pl.semaphore_signal(barrier, inc=1, device_id={"tm": 1 - tm, "height": h + dz})
        count = count + 2 * there(dz).astype(jnp.int32)

    for d in range(groups):
        total = None
        for j in range(groups):
            hit = (route_ref[clip * groups + j] == d).astype(F32)
            term = pix_ref[j].astype(F32) * hit
            total = term if total is None else total + term
        for f in range(total.shape[1]):
            send[d, f] = total[:, f, :].astype(BF16)
    out_ref[1, 2, clip] = send[clip]
    zero = jnp.zeros(out_ref.shape[2:], BF16)
    for k in range(5):
        lost = jnp.logical_not(there(k - 2))

        @pl.when(jnp.logical_or(lost, tm == 0))
        def _(k=k):
            out_ref[0, k] = zero
        if k != 2:
            @pl.when(lost)
            def _(k=k):
                out_ref[1, k] = zero

    pl.semaphore_wait(barrier, count)
    first = []
    for k in range(1, groups):
        d = lax.rem(clip + k, groups)
        copy = pltpu.make_async_remote_copy(
            send.at[d], out_ref.at[1, 2, clip], s1.at[k], r1.at[k],
            device_id={"clip": d})
        copy.start()
        first.append(copy)
    for k in range(1, groups):
        source = lax.rem(clip + groups - k, groups)
        pltpu.make_async_remote_copy(
            send.at[0], out_ref.at[1, 2, source], s1.at[k], r1.at[k],
            device_id={"clip": source}).wait_recv()

    def out_going(j, dz):
        place = {"height": h + dz} if j == 1 else {"tm": 1 - tm, "height": h + dz}
        return pltpu.make_async_remote_copy(
            out_ref.at[1, 2], out_ref.at[j, 2 - dz], s2.at[j, 2 - dz], r2.at[j, 2 - dz],
            device_id=place)

    def in_coming(j, k):
        return pltpu.make_async_remote_copy(
            out_ref.at[1, 2], out_ref.at[j, k], s2.at[j, k], r2.at[j, k],
            device_id={"tm": 1 - tm})

    hops = [(0, 0)] + [(j, dz) for dz in (1, -1, 2, -2) for j in (0, 1)]
    for j, dz in hops:
        @pl.when(jnp.logical_and(there(dz), jnp.logical_or(j == 1, tm == 0)))
        def _(j=j, dz=dz):
            out_going(j, dz).start()
    prepare()
    for copy in first:
        copy.wait_send()
    for j, dz in hops:
        @pl.when(jnp.logical_and(there(dz), jnp.logical_or(j == 1, tm == 1)))
        def _(j=j, dz=dz):
            in_coming(j, 2 + dz).wait_recv()
    for j, dz in hops:
        @pl.when(jnp.logical_and(there(dz), jnp.logical_or(j == 1, tm == 0)))
        def _(j=j, dz=dz):
            out_going(j, dz).wait_send()


def kernel(groups, heights, lengths_ref, route_ref, own_ref, taps_hbm, b_in_ref, gain_ref, b_mid_ref, w2_hbm, out_ref,
           pix_ref, taps_ref, w2_ref, grid, cols, acts, wide, tall, w1_ref, rows, loaded, *sent):
    load_taps = pltpu.make_async_copy(taps_hbm, taps_ref, loaded.at[0])
    load_w2 = pltpu.make_async_copy(w2_hbm, w2_ref, loaded.at[1])
    load_taps.start()
    load_w2.start()
    ch = b_in_ref.shape[1]
    width = pix_ref.shape[-1]
    clip = lax.axis_index("clip")
    tm = lax.axis_index("tm")
    h = lax.axis_index("height")
    lane = lax.broadcasted_iota(jnp.int32, (1, width), 1)
    rows[...] = jnp.zeros_like(rows)
    for n, row in enumerate((b_in_ref, gain_ref, b_mid_ref)):
        rows[n:n + 1, :ch] = row[...]
    par = rows[...].T[:ch]
    b_in, gain, b_mid = par[:, 0:1], par[:, 1:2], par[:, 2:3]

    def right(v):
        return jnp.where(lane == 0, 0.0, pltpu.roll(v, 1, 1))

    def left(v):
        return jnp.where(lane == width - 1, 0.0, pltpu.roll(v, width - 1, 1))

    def prepare():
        load_taps.wait()
        tall[...] = jnp.zeros_like(tall)
        for i in range(3):
            for dt in range(3):
                for dr in range(3):
                    piece = taps_ref[i, dt, dr].astype(F32)
                    for r in range(3):
                        for dc in range(3):
                            at = dt * 48 + dc * 16 + (r + dr) * 3 + i
                            tall[at:at + 1, r * 128:r * 128 + ch] = piece[dc:dc + 1]
        for r in range(3):
            w1_ref[r * ch:(r + 1) * ch, :] = tall[:, r * 128:(r + 1) * 128].T[:ch].astype(BF16)
        load_w2.wait()
        wide[...] = jnp.zeros_like(wide)
        for dt in range(3):
            for dr in range(3):
                for dc in range(3):
                    at = (dt * 3 + dr) * 128
                    wide[dc * ch:(dc + 1) * ch, at:at + ch] = w2_ref[dt, dr, dc]

    gather(groups, heights, prepare, route_ref, own_ref, pix_ref, *sent)

    def one(c, carry):
        grid[...] = jnp.zeros_like(grid)
        for j in range(2):
            for k in range(5):
                for f in range(2):
                    grid[2 + 2 * j + f, 3 * k:3 * k + 3, :] = pix_ref[j, k, c, f].astype(F32)
        for p in range(6):
            v = grid[p]
            cols[p * 48:p * 48 + 16, :] = right(v).astype(BF16)
            cols[p * 48 + 16:p * 48 + 32, :] = v.astype(BF16)
            cols[p * 48 + 32:p * 48 + 48, :] = left(v).astype(BF16)
        kept = []
        pad = jnp.zeros((128 - ch, width), BF16)
        for f in range(4):
            s = jnp.dot(w1_ref[...], cols[f * 48:f * 48 + 144, :], preferred_element_type=F32)
            for r in range(3):
                stem = (s[r * ch:(r + 1) * ch] + b_in).astype(BF16).astype(F32)
                scale = lax.rsqrt(jnp.mean(stem * stem, axis=0, keepdims=True) + 1e-6)
                v = 0.5 * (stem * scale * gain)
                act = v + v * jnp.tanh(v)
                live = jnp.logical_and(h - 1 + r >= 0, h - 1 + r < heights)
                if f < 2:
                    live = jnp.logical_and(live, tm > 0)
                at = (f * 3 + r) * 128
                acts[at:at + ch, :] = jnp.where(live, act, 0.0).astype(BF16)
                acts[at + ch:at + 128, :] = pad
                if f >= 2 and r == 1:
                    kept.append(stem)
        length = 0
        for j in range(groups):
            q = c * groups + j
            length = length + jnp.where(route_ref[q] == clip, lengths_ref[q], 0)
        for t in range(2):
            y = jnp.dot(wide[...], acts[t * 384:t * 384 + 1152, :], preferred_element_type=F32)
            o = y[ch:2 * ch] + right(y[:ch]) + left(y[2 * ch:]) + b_mid + kept[t]
            out_ref[c, t] = jnp.where(tm * 2 + t < length, o, 0.0).astype(BF16)
        return carry

    lax.fori_loop(0, groups, one, 0)


def local(groups, heights, pixels, lengths, route, w_in, b_in, gain, w_mid, b_mid):
    clips, colours, frames, _, width = pixels.shape
    ch = w_in.shape[0]
    vmem = pl.BlockSpec(memory_space=pltpu.VMEM)
    hbm = pl.BlockSpec(memory_space=pltpu.HBM)
    smem = pl.BlockSpec(memory_space=pltpu.SMEM)
    pix = pixels.reshape(clips, colours, frames, width)
    w1 = jnp.transpose(w_in, (1, 2, 3, 4, 0))
    rows = [v.reshape(1, ch) for v in (b_in, gain, b_mid)]
    w2 = jnp.transpose(w_mid, (2, 3, 4, 0, 1))
    out = pl.pallas_call(
        functools.partial(kernel, groups, heights),
        out_shape=pltpu.VMEM((clips, frames, ch, width), BF16),
        in_specs=[smem, smem, vmem, hbm, vmem, vmem, vmem, hbm],
        out_specs=vmem,
        scratch_shapes=[
            pltpu.VMEM((2, 5, clips, frames, colours, width), BF16),
            pltpu.VMEM(w1.shape, BF16),
            pltpu.VMEM(w2.shape, BF16),
            pltpu.VMEM((6, 16, width), F32),
            pltpu.VMEM((288, width), BF16),
            pltpu.VMEM((12 * 128, width), BF16),
            pltpu.VMEM((3 * ch, 9 * 128), BF16),
            pltpu.VMEM((144, 3 * 128), F32),
            pltpu.VMEM((3 * ch, 144), BF16),
            pltpu.VMEM((8, 128), F32),
            pltpu.SemaphoreType.DMA((2,)),
            pltpu.VMEM((groups, frames, colours, width), BF16),
            pltpu.SemaphoreType.DMA((groups,)),
            pltpu.SemaphoreType.DMA((groups,)),
            pltpu.SemaphoreType.DMA((2, 5)),
            pltpu.SemaphoreType.DMA((2, 5)),
        ],
        compiler_params=pltpu.CompilerParams(collective_id=0, has_side_effects=True, vmem_limit_bytes=56 * 1024 * 1024),
    )(lengths, route, pix, w1, *rows, w2)
    return jnp.transpose(out, (0, 2, 1, 3))[:, :, :, None, :]


def solution(mesh):
    placed = (P("clip", None, "tm", "height", None), P(), P(), P(), P(), P(), P(), P())
    return jax.shard_map(
        functools.partial(local, mesh.shape["clip"], mesh.shape["height"]),
        mesh=mesh,
        in_specs=placed,
        out_specs=P("clip", None, "tm", "height", None),
        check_vma=False,
    )
```
